256 devices in a mesh: segment: 8 (over z), neuron: 32 (over x, y, core).
Axes of the slice: x: 4, y: 4, z: 8, core: 2. Of those that a mesh axis runs over, the one named last changes fastest.
Arguments:
- samples: bfloat16 [4, 128, 65536], P(None, None, 'neuron'), may hold values from -48 to 48
- weights: bfloat16 [16, 65536, 256], P('segment', 'neuron'), may hold values from -0.5 to 0.5
- biases: bfloat16 [16, 65536], P('segment', 'neuron'), may hold values from -12 to 12
- near_blocks: int32 [16, 1024, 3], P('segment', 'neuron'), may hold values from 0 to 31
- remote_cols: int32 [16, 1024], P('segment'), may hold values from 0 to 1023, as said below
Outputs:
- activations: bfloat16 [4, 128, 65536], P(None, 'segment', 'neuron')
The draws below stay inside these ranges and needn't reach their ends.
Inputs may be any that keep to these rules, and one draw needn't show every extreme that they name: In every layer, the 32 output blocks of one index of neuron (blocks 32 p to 32 p + 31) name remote columns whose owner remote_cols // 32 is named by exactly 0 or exactly 2 of those blocks.
All inputs are finite; a program needn't handle non-finite values.
Results may differ from the reference program's by a relative error of at most 0.028.
Values may be sent and summed in bfloat16 or wider, within the bound.
A program may use at most 128 MiB of HBM per device.

```python
import jax
import jax.numpy as jnp
from jax import lax

NEURONS = 65536
KL = 3
MB = 4
MBROWS = 128
LAYERS = 16
NBLK = 1024
BR = 32
CAP = 2


def draw_remote_cols(key, part):
    key = jax.random.fold_in(key, 7)
    owners_count = NBLK // BR
    keys = jax.random.split(key, LAYERS * owners_count)

    def one_block(single):
        first, second, third = jax.random.split(single, 3)
        owners = jax.random.permutation(first, owners_count)[:BR // CAP]
        listed = jnp.repeat(owners, CAP, total_repeat_length=BR)
        listed = jax.random.permutation(second, listed)
        inside = jax.random.randint(third, (BR,), 0, BR)
        return listed * BR + inside
    return jax.vmap(one_block)(keys).reshape(LAYERS, NBLK).astype(jnp.int32)


def set_ends(drawn, rng, smallest, top_value):
    place = [jax.random.randint(jax.random.fold_in(rng, axis), (), 0, length) for axis, length in enumerate(drawn.shape)]
    main_axis = drawn.shape.index(max(drawn.shape))
    neighbour = place[:main_axis] + [(place[main_axis] + 1) % drawn.shape[main_axis]] + place[main_axis + 1:]
    return drawn.at[tuple(place)].set(smallest).at[tuple(neighbour)].set(top_value)


def block_scale(rng, extent, pieces, least, largest):
    def one(dim, parts):
        draws = jax.random.uniform(jax.random.fold_in(jax.random.fold_in(rng, 6), dim), (parts,), jnp.float32, least / len(pieces), largest / len(pieces))
        return jnp.repeat(jnp.exp(draws), extent[dim] // parts).reshape((-1,) + (1,) * (len(extent) - dim - 1))

    loudness = one(*pieces[0])
    for cut in pieces[1:]:
        loudness = loudness * one(*cut)
    return loudness


def normal_values(rng, extent, deviation, bound, shards=(), held_as=jnp.bfloat16):
    result = jax.random.normal(rng, extent, jnp.float32) * deviation
    if len(shards) > 0:
        result = block_scale(rng, extent, shards, -0.22, 0.18) * result
    return jnp.clip(result, min=-bound, max=bound).astype(held_as)


def setup_inputs(seed: int = 0) -> dict:
    arg_keys = jax.random.split(jax.random.key(seed), 6)
    return {
        "samples": normal_values(arg_keys[0], (MB, MBROWS, NEURONS), 8.0, 48.0, ((2, 32),)),
        "weights": normal_values(arg_keys[1], (LAYERS, NEURONS, KL * 64 + 64), ((KL * 64 + 64) // 2) ** -0.5, 0.5, ((0, 8), (1, 32))),
        "biases": normal_values(arg_keys[2], (LAYERS, NEURONS), 2.0, 12.0, ((0, 8), (1, 32))),
        "near_blocks": set_ends(jax.random.randint(arg_keys[3], (LAYERS, NBLK, KL), 0, BR), jax.random.fold_in(arg_keys[3], 1), 0, BR - 1).astype(jnp.int32),
        "remote_cols": draw_remote_cols(jax.random.fold_in(arg_keys[5], 71), 0),
    }


def reference(samples, weights, biases, near_blocks, remote_cols):
    base = (jnp.arange(NBLK, dtype=jnp.int32) // BR) * BR
    columns = jnp.concatenate([near_blocks + base[None, :, None], remote_cols[:, :, None]], axis=2).astype(jnp.int32)

    def layer(act, packed):
        weight, bias, cols = packed
        rows = act.shape[0]
        blocks = act.reshape(rows, NBLK, 64)
        taken = blocks[:, cols].reshape(rows, NBLK, (KL + 1) * 64)
        shaped = weight.reshape(NBLK, 64, (KL + 1) * 64)
        total = jnp.einsum("sbk,bok->sbo", taken.astype(jnp.float32), shaped.astype(jnp.float32))
        total = total.reshape(rows, NEURONS) + bias.astype(jnp.float32)[None, :]
        return jnp.clip(total, 0.0, 32.0).astype(jnp.bfloat16), None

    results = []
    for batch in range(MB):
        final, _ = lax.scan(layer, samples[batch], (weights, biases, columns))
        results.append(final)
    return jnp.stack(results)
```

```python
import functools

import jax
import jax.numpy as jnp
from jax import lax
from jax.experimental import pallas as pl
from jax.experimental.pallas import tpu as pltpu
from jax.sharding import PartitionSpec as P

MESH = pl.DeviceIdType.MESH
BLK = 64
CHUNKS = 8
SKEW = 2
GROUP = 8


def tables(cols, near, owners, me):
    layers = cols.shape[0]
    grid = cols.reshape(layers, owners, -1)
    per = grid.shape[2]
    place = lax.broadcasted_iota(jnp.int32, grid.shape, 2)
    asked = (grid // per) == me
    first = jnp.min(jnp.where(asked, place, per - 1), axis=2, keepdims=True)
    last = jnp.max(jnp.where(asked, place, 0), axis=2, keepdims=True)
    inside = grid % per
    send = jnp.concatenate(
        [
            jnp.sum(jnp.where(place == first, inside, 0), axis=2),
            jnp.sum(jnp.where(place == last, inside, 0), axis=2),
        ],
        axis=1,
    )
    mine = lax.dynamic_index_in_dim(grid, me, 1, keepdims=False) // per
    same = mine[:, :, None] == mine[:, None, :]
    earlier = lax.broadcasted_iota(jnp.int32, same.shape, 2) < lax.broadcasted_iota(
        jnp.int32, same.shape, 1
    )
    slot = jnp.max(jnp.where(same & earlier, 1, 0), axis=2)
    row = lambda v: jnp.pad(v, ((0, 0), (0, 128 - v.shape[1])))
    far = jnp.concatenate([mine, slot], axis=1)
    packed = jnp.stack(
        [row(send), row(near.reshape(layers, -1)), row(far), jnp.zeros((layers, 128), jnp.int32)],
        axis=1,
    )
    return packed.reshape(layers * 4, 128)


def kernel(
    dims, x_ref, w_ref, b_ref, t_ref, o_ref,
    act_even, act_odd, total, send, recv_even, recv_odd, wbuf, ball, btr, tall, tabs,
    local_sem, small_send, small_recv, a2a_send, a2a_recv, ring_send, ring_recv,
):
    sections, owners, per, layers, rows = dims
    own = layers // sections
    half = per // 2
    step = half // CHUNKS
    s = lax.axis_index("segment")
    me = lax.axis_index("neuron")
    ahead = lax.rem(s + 1, sections)
    behind = lax.rem(s + sections - 1, sections)
    last = sections - 1

    loads = [
        pltpu.make_async_copy(x_ref, act_even, local_sem.at[0]),
        pltpu.make_async_copy(w_ref, wbuf.at[pl.ds(s * own, own)], local_sem.at[1]),
    ]
    for load in loads:
        load.start()
    tall[pl.ds(s, 1)] = t_ref[...][None]
    ball[pl.ds(s * own, own)] = b_ref[...]

    barrier = pltpu.get_barrier_semaphore()

    def greet(d, carry):
        pl.semaphore_signal(
            barrier, inc=1, device_id={"neuron": lax.rem(me + d, owners)}, device_id_type=MESH
        )
        return carry

    lax.fori_loop(1, owners, greet, 0)

    def greet_section(d, carry):
        pl.semaphore_signal(
            barrier, inc=1, device_id={"segment": lax.rem(s + d, sections)}, device_id_type=MESH
        )
        return carry

    lax.fori_loop(1, sections, greet_section, 0)
    pl.semaphore_wait(barrier, owners - 1 + sections - 1)

    def share(d, carry):
        to = {"segment": lax.rem(s + d, sections)}
        pltpu.make_async_remote_copy(
            src_ref=tall.at[pl.ds(s, 1)], dst_ref=tall.at[pl.ds(s, 1)],
            send_sem=small_send.at[0], recv_sem=small_recv.at[0],
            device_id=to, device_id_type=MESH,
        ).start()
        pltpu.make_async_remote_copy(
            src_ref=ball.at[pl.ds(s * own, own)], dst_ref=ball.at[pl.ds(s * own, own)],
            send_sem=small_send.at[1], recv_sem=small_recv.at[1],
            device_id=to, device_id_type=MESH,
        ).start()
        return carry

    lax.fori_loop(1, sections, share, 0)

    def ring(source, layer, part, side, to):
        at = pl.ds(side * half + part * step, step)
        return pltpu.make_async_remote_copy(
            src_ref=source.at[at], dst_ref=wbuf.at[layer, at],
            send_sem=ring_send.at[side, layer], recv_sem=ring_recv.at[side, layer, part],
            device_id={"segment": to}, device_id_type=MESH,
        )

    def start_own(i, carry):
        t, part = i // CHUNKS, i % CHUNKS
        ring(w_ref.at[t], s * own + t, part, 0, ahead).start()
        ring(w_ref.at[t], s * own + t, part, 1, behind).start()
        return carry

    lax.fori_loop(0, own * CHUNKS, start_own, 0)

    parts = own * CHUNKS
    wide, tight = parts + SKEW, parts - SKEW

    def hand_on(k, side, to, fine, far_off):
        copy = ring(wbuf.at[k // CHUNKS], k // CHUNKS, lax.rem(k, CHUNKS), side, to)

        @pl.when(fine)
        def _():
            copy.wait_recv()

        @pl.when(fine & (far_off < last))
        def _():
            copy.start()

    def ring_step(e):
        t = e - SKEW * s
        early = t < tight * s + SKEW
        t = jnp.where(early, t, t - SKEW * sections)
        low, high = jnp.where(early, 0, s + 1), jnp.where(early, s, sections)
        h = jnp.maximum(t, 0) // tight
        rest = t - h * tight
        for home, fits in ((h - 1, rest < SKEW), (h, t >= 0)):
            fine = fits & (home >= low) & (home < high)
            k = jnp.clip(t + SKEW * home, 0, parts * sections - 1)
            hand_on(k, 0, ahead, fine, lax.rem(s - home + sections, sections))
        t = e + SKEW * s
        early = t < wide * s + tight
        t = jnp.where(early, t - SKEW * sections, t)
        low, high = jnp.where(early, 0, s + 1), jnp.where(early, s, sections)
        h = jnp.maximum(t, 0) // wide
        fine = (t >= 0) & (t - h * wide < parts) & (h >= low) & (h < high)
        k = jnp.clip(t - SKEW * h, 0, parts * sections - 1)
        hand_on(k, 1, behind, fine, lax.rem(h - s + sections, sections))

    def ring_steps(low, count):
        def one(i, carry):
            ring_step(low + i)
            return carry

        lax.fori_loop(0, count, one, 0)

    pltpu.make_async_copy(
        tall.at[pl.ds(0, sections - 1)], tall.at[pl.ds(0, sections - 1)], small_recv.at[0]
    ).wait()
    table_load = pltpu.make_async_copy(tall, tabs, local_sem.at[2])
    table_load.start()
    pltpu.make_async_copy(
        ball.at[pl.ds(0, layers - own)], ball.at[pl.ds(0, layers - own)], small_recv.at[1]
    ).wait()
    for i in range(per // 2):
        rows_of = jnp.concatenate(
            [
                jnp.zeros((BLK, 128), jnp.float32),
                ball[:, i, :],
                jnp.zeros((BLK - layers, 128), jnp.float32),
            ],
            axis=0,
        )
        btr[2 * i : 2 * i + 2] = rows_of.T.astype(jnp.bfloat16).reshape(2, BLK, 128)
    table_load.wait()
    for load in loads:
        load.wait()

    low_lanes = lax.broadcasted_iota(jnp.int32, (BLK, 128), 1) < BLK
    lead = SKEW * last + CHUNKS

    def one_layer(layer, now):
        act, after = (act_even, act_odd)[now], (act_odd, act_even)[now]
        recv = (recv_even, recv_odd)[now]
        home, base = layer // own, lax.rem(layer, own) * 4
        step_at = lead + layer * CHUNKS

        @pl.when(layer >= 2)
        def _():
            sent = send.at[now, pl.ds(0, owners - 1)]
            pltpu.make_async_copy(sent, sent, a2a_send.at[now]).wait()

        def pair(q):
            first = tabs[home, base, q]
            second = tabs[home, base, owners + q]
            return jnp.where(low_lanes, act[first], act[second])

        def give(d, c):
            q = lax.rem(me + d, owners)
            send[now, q] = pair(q)
            pltpu.make_async_remote_copy(
                src_ref=send.at[now, q], dst_ref=recv.at[me],
                send_sem=a2a_send.at[now], recv_sem=a2a_recv.at[now],
                device_id={"neuron": q}, device_id_type=MESH,
            ).start()
            return c

        lax.fori_loop(1, owners, give, 0)
        recv[me] = pair(me)

        @pl.when(layer == 0)
        def _():
            ring_steps(0, lead)

        ring_steps(step_at, CHUNKS // 4)
        pick = jnp.where(
            lax.broadcasted_iota(jnp.int32, (BLK, 128), 0) == layer, 1.0, 0.0
        ).astype(jnp.bfloat16)

        def near_group(g, c):
            joined, packed = [], []
            for i in range(GROUP):
                j = g * GROUP + i
                near = [act[tabs[home, base + 1, 3 * j + k]] for k in range(3)]
                joined.append(jnp.concatenate(near + [pick], axis=0))
                w = wbuf[layer, j]
                packed.append(
                    jnp.concatenate(
                        [w[:, :128], jnp.where(low_lanes, w[:, 128:], btr[j])], axis=1
                    )
                )
            sums = [
                jnp.dot(p, x, preferred_element_type=jnp.float32) for p, x in zip(packed, joined)
            ]
            for i in range(GROUP):
                total[g * GROUP + i] = sums[i]
            return c

        groups = per // GROUP

        def near_and_feed(g, c):
            near_group(g, c)
            ring_step(step_at + CHUNKS // 4 + g)
            return c

        fed = min(groups, CHUNKS // 2)
        lax.fori_loop(0, fed, near_and_feed, 0)
        lax.fori_loop(fed, groups, near_group, 0)
        got = recv.at[pl.ds(0, owners - 1)]
        pltpu.make_async_copy(got, got, a2a_recv.at[now]).wait()

        def far_group(g, c):
            pairs, straights, sums, done = [], [], [], []
            for i in range(GROUP):
                j = g * GROUP + i
                pairs.append(recv[tabs[home, base + 2, j]])
                slot = jnp.zeros((BLK, 128), jnp.int32) + tabs[home, base + 2, per + j]
                straights.append(low_lanes == (slot == 0))
            for i in range(GROUP):
                joined = jnp.concatenate([jnp.zeros((BLK, 128), jnp.bfloat16), pairs[i]], axis=0)
                w = wbuf[layer, g * GROUP + i][:, 128:]
                sums.append(jnp.dot(w, joined, preferred_element_type=jnp.float32))
            for i in range(GROUP):
                far = jnp.where(straights[i], sums[i], pltpu.roll(sums[i], BLK, 1))
                z = total[g * GROUP + i] + far
                done.append(jnp.minimum(jnp.maximum(z, 0.0), 32.0).astype(jnp.bfloat16))
            for i in range(GROUP):
                after[g * GROUP + i] = done[i]
            return c

        lax.fori_loop(0, groups // 2, far_group, 0)
        ring_step(step_at + CHUNKS - CHUNKS // 4)
        lax.fori_loop(groups // 2, groups, far_group, 0)
        ring_steps(step_at + CHUNKS - CHUNKS // 4 + 1, CHUNKS // 4 - 1)

    def two_layers(i, carry):
        one_layer(2 * i, 0)
        one_layer(2 * i + 1, 1)
        return carry

    lax.fori_loop(0, layers // 2, two_layers, 0)
    o_ref[...] = act_even[...]

    for par in range(2):
        sent = send.at[par, pl.ds(0, owners - 1)]
        pltpu.make_async_copy(sent, sent, a2a_send.at[par]).wait()

    def drain(layer, carry):
        home = layer // own
        for side, gone in (
            (0, lax.rem(s - home + sections, sections)),
            (1, lax.rem(home - s + sections, sections)),
        ):

            @pl.when(gone < last)
            def _():
                sent = wbuf.at[layer, pl.ds(side * half, half)]
                pltpu.make_async_copy(sent, sent, ring_send.at[side, layer]).wait()

        return carry

    lax.fori_loop(0, layers, drain, 0)
    out = tall.at[pl.ds(0, sections - 1)]
    pltpu.make_async_copy(out, out, small_send.at[0]).wait()
    out = ball.at[pl.ds(0, layers - own)]
    pltpu.make_async_copy(out, out, small_send.at[1]).wait()


def local(samples, weights, biases, near_blocks, remote_cols):
    batches, rows, width = samples.shape
    sections = lax.axis_size("segment")
    owners = lax.axis_size("neuron")
    s = lax.axis_index("segment")
    me = lax.axis_index("neuron")
    per = width // BLK
    own = weights.shape[0]
    layers = own * sections
    share = rows // sections
    count = batches * share
    mine = lax.dynamic_slice_in_dim(samples, s * share, share, 1).reshape(count, width)
    x = mine.T
    x = jnp.concatenate([x, x], axis=1).reshape(per, BLK, 128)
    table = tables(remote_cols, near_blocks, owners, me)
    bias = biases.astype(jnp.float32).reshape(own, width // 128, 128)
    dims = (sections, owners, per, layers, count)
    bf16, f32 = jnp.bfloat16, jnp.float32
    out = pl.pallas_call(
        functools.partial(kernel, dims),
        out_shape=jax.ShapeDtypeStruct((per, BLK, 128), bf16),
        in_specs=[
            pl.BlockSpec(memory_space=pl.ANY),
            pl.BlockSpec(memory_space=pl.ANY),
            pl.BlockSpec(memory_space=pltpu.VMEM),
            pl.BlockSpec(memory_space=pltpu.VMEM),
        ],
        out_specs=pl.BlockSpec(memory_space=pltpu.VMEM),
        scratch_shapes=[
            pltpu.VMEM((per, BLK, 128), bf16),
            pltpu.VMEM((per, BLK, 128), bf16),
            pltpu.VMEM((per, BLK, 128), f32),
            pltpu.VMEM((2, owners, BLK, 128), bf16),
            pltpu.VMEM((owners, BLK, 128), bf16),
            pltpu.VMEM((owners, BLK, 128), bf16),
            pltpu.VMEM((layers, per, BLK, 256), bf16),
            pltpu.VMEM((layers, width // 128, 128), f32),
            pltpu.VMEM((per, BLK, 128), bf16),
            pltpu.VMEM((sections, own * 4, 128), jnp.int32),
            pltpu.SMEM((sections, own * 4, 128), jnp.int32),
            pltpu.SemaphoreType.DMA((3,)),
            pltpu.SemaphoreType.DMA((2,)),
            pltpu.SemaphoreType.DMA((2,)),
            pltpu.SemaphoreType.DMA((2,)),
            pltpu.SemaphoreType.DMA((2,)),
            pltpu.SemaphoreType.DMA((2, layers)),
            pltpu.SemaphoreType.DMA((2, layers, CHUNKS)),
        ],
        compiler_params=pltpu.CompilerParams(
            collective_id=0, has_side_effects=True, vmem_limit_bytes=48 * 1024 * 1024
        ),
    )(x, weights.reshape(own, per, BLK, 256), bias, table)
    y = out.reshape(width, 128)[:, :count].T
    return y.reshape(batches, share, width)


def solution(mesh):
    return jax.shard_map(
        local,
        mesh=mesh,
        in_specs=(
            P(None, None, "neuron"),
            P("segment", "neuron", None),
            P("segment", "neuron"),
            P("segment", "neuron", None),
            P("segment", None),
        ),
        out_specs=P(None, "segment", "neuron"),
        check_vma=False,
    )
```

```python
import functools

import jax
import jax.numpy as jnp
from jax import lax
from jax.experimental import pallas as pl
from jax.experimental.pallas import tpu as pltpu
from jax.sharding import PartitionSpec as P

MESH = pl.DeviceIdType.MESH
BLK = 64
UNIT = 2
FIRST_SHARE = 8
SECOND_SHARE = 7
SKEW = 3
LEAD = 31
BEHIND = 5
GROUP = 8


def tables(cols, near, owners, me):
    layers = cols.shape[0]
    grid = cols.reshape(layers, owners, -1)
    per = grid.shape[2]
    place = lax.broadcasted_iota(jnp.int32, grid.shape, 2)
    asked = (grid // per) == me
    first = jnp.min(jnp.where(asked, place, per - 1), axis=2, keepdims=True)
    last = jnp.max(jnp.where(asked, place, 0), axis=2, keepdims=True)
    inside = grid % per
    send = jnp.concatenate(
        [
            jnp.sum(jnp.where(place == first, inside, 0), axis=2),
            jnp.sum(jnp.where(place == last, inside, 0), axis=2),
        ],
        axis=1,
    )
    mine = lax.dynamic_index_in_dim(grid, me, 1, keepdims=False) // per
    same = mine[:, :, None] == mine[:, None, :]
    earlier = lax.broadcasted_iota(jnp.int32, same.shape, 2) < lax.broadcasted_iota(
        jnp.int32, same.shape, 1
    )
    slot = jnp.max(jnp.where(same & earlier, 1, 0), axis=2)
    row = lambda v: jnp.pad(v, ((0, 0), (0, 128 - v.shape[1])))
    far = jnp.concatenate([mine, slot], axis=1)
    packed = jnp.stack(
        [row(send), row(near.reshape(layers, -1)), row(far), jnp.zeros((layers, 128), jnp.int32)],
        axis=1,
    )
    return packed.reshape(layers * 4, 128)


def kernel(
    dims, x_ref, w_ref, b_ref, t_ref, o_ref,
    act_even, act_odd, total, send, recv_even, recv_odd, wbuf, ball, btr, tall, tabs,
    local_sem, small_send, small_recv, a2a_send, a2a_recv, ring_send, ring_recv,
):
    sections, owners, per, layers, rows = dims
    own = layers // sections
    s = lax.axis_index("segment")
    me = lax.axis_index("neuron")
    ahead = lax.rem(s + 1, sections)
    behind = lax.rem(s + sections - 1, sections)
    last = sections - 1

    loads = [
        pltpu.make_async_copy(x_ref, act_even, local_sem.at[0]),
        pltpu.make_async_copy(w_ref, wbuf.at[pl.ds(s * own, own)], local_sem.at[1]),
    ]
    for load in loads:
        load.start()
    tall[pl.ds(s, 1)] = t_ref[...][None]
    ball[pl.ds(s * own, own)] = b_ref[...]

    barrier = pltpu.get_barrier_semaphore()

    def greet(d, carry):
        pl.semaphore_signal(
            barrier, inc=1, device_id={"neuron": lax.rem(me + d, owners)}, device_id_type=MESH
        )
        return carry

    lax.fori_loop(1, owners, greet, 0)

    def greet_section(d, carry):
        pl.semaphore_signal(
            barrier, inc=1, device_id={"segment": lax.rem(s + d, sections)}, device_id_type=MESH
        )
        return carry

    lax.fori_loop(1, sections, greet_section, 0)
    pl.semaphore_wait(barrier, owners - 1 + sections - 1)

    def share(d, carry):
        to = {"segment": lax.rem(s + d, sections)}
        pltpu.make_async_remote_copy(
            src_ref=tall.at[pl.ds(s, 1)], dst_ref=tall.at[pl.ds(s, 1)],
            send_sem=small_send.at[0], recv_sem=small_recv.at[0],
            device_id=to, device_id_type=MESH,
        ).start()
        pltpu.make_async_remote_copy(
            src_ref=ball.at[pl.ds(s * own, own)], dst_ref=ball.at[pl.ds(s * own, own)],
            send_sem=small_send.at[1], recv_sem=small_recv.at[1],
            device_id=to, device_id_type=MESH,
        ).start()
        return carry

    lax.fori_loop(1, sections, share, 0)

    units = per // UNIT
    first = (FIRST_SHARE, units - FIRST_SHARE)
    second = (SECOND_SHARE, units - SECOND_SHARE)
    window = (first[0] + second[0], first[1] + second[1])
    lone = window[0] - SKEW
    end = window[1] * sections

    def ring(source, home, i, side, to, own_source):
        later = (i >= first[side]).astype(jnp.int32)
        begin = 0 if side == 0 else first[0] + later * (second[0] - first[0])
        place = begin + i - later * first[side]
        at = pl.ds(place * UNIT, UNIT)
        layer = home * own + later
        return pltpu.make_async_remote_copy(
            src_ref=source.at[later if own_source else layer, at], dst_ref=wbuf.at[layer, at],
            send_sem=ring_send.at[side, later], recv_sem=ring_recv.at[side, home, i],
            device_id={"segment": to}, device_id_type=MESH,
        )

    def hand_on(side, home, i, fine, hops):
        home, i = jnp.clip(home, 0, last), jnp.clip(i, 0, window[side] - 1)
        copy = ring(wbuf, home, i, side, (ahead, behind)[side], False)

        @pl.when(fine)
        def _():
            copy.wait_recv()

        @pl.when(fine & (hops < last))
        def _():
            copy.start()

    own_base = jnp.where(s == last, SKEW * (last - 1), window[0] * s)
    own_early = jnp.where(s == 0, window[1], jnp.minimum(window[1], SKEW * (sections - s)))
    own_late = window[1] * (s - 1) + SKEW * (sections - s) - own_early

    def give_own(side, i, fine):
        @pl.when(fine)
        def _():
            i_in = jnp.clip(i, 0, window[side] - 1)
            ring(w_ref, s, i_in, side, (ahead, behind)[side], True).start()

    def ring_step(e):
        t = e - own_base
        give_own(0, jnp.where(e < SKEW, e, t), (e < SKEW) | ((t >= SKEW) & (t < window[0])))
        t = e - own_late
        give_own(
            1,
            jnp.where(e < own_early, e, t),
            (e < own_early) | ((s > 0) & (t >= own_early) & (t < window[1])),
        )

        inner = (e >= SKEW) & (e < SKEW * s)
        home = jnp.where(inner, s - e // SKEW, -1)
        i = lax.rem(e, SKEW)
        t = e - SKEW * s
        fits = (s >= 1) & (t >= 0) & (t < window[0])
        home, i = jnp.where(fits, 0, home), jnp.where(fits, t, i)
        t = t - window[0]
        fits = (t >= 0) & (t < lone * (s - 1))
        t = jnp.maximum(t, 0)
        home = jnp.where(fits, 1 + t // lone, home)
        i = jnp.where(fits, SKEW + lax.rem(t, lone), i)
        t = e - window[0] * (s + 1)
        fits = (t >= 0) & (t < SKEW * (last - 1 - s))
        t_in = jnp.maximum(t, 0)
        home = jnp.where(fits, last - 1 - t_in // SKEW, home)
        i = jnp.where(fits, lax.rem(t_in, SKEW), i)
        t = t - SKEW * (last - 1 - s)
        fits = (s < last) & (t >= 0) & (t < window[0])
        home, i = jnp.where(fits, last, home), jnp.where(fits, t, i)
        hand_on(0, home, i, home >= 0, lax.rem(s - home + sections, sections))

        t = e - SKEW * (sections + 1 + s)
        t_in = jnp.maximum(t, 0)
        home = t_in // lone
        fine = (t >= 0) & (home > s) & (home < last)
        hand_on(0, home, SKEW + lax.rem(t_in, lone), fine, s - home + sections)

        for t, low, high, hops in (
            (e - SKEW * (sections - s), 0, s, sections - s),
            (e + SKEW * s, s + 1, sections, -s),
        ):
            t_in = jnp.maximum(t, 0)
            home = t_in // window[1]
            fine = (t >= 0) & (home >= low) & (home < high)
            hand_on(1, home, lax.rem(t_in, window[1]), fine, home + hops)

    def ring_until(low, high):
        def one(e, carry):
            ring_step(e)
            return carry

        lax.fori_loop(low, high, one, 0)
        return jnp.maximum(low, high)

    def needed(layer):
        return jnp.minimum(LEAD + layer * (end + BEHIND - LEAD) // (layers - 1), end)

    done = ring_until(0, SKEW)
    pltpu.make_async_copy(
        tall.at[pl.ds(0, sections - 1)], tall.at[pl.ds(0, sections - 1)], small_recv.at[0]
    ).wait()
    table_load = pltpu.make_async_copy(tall, tabs, local_sem.at[2])
    table_load.start()
    pltpu.make_async_copy(
        ball.at[pl.ds(0, layers - own)], ball.at[pl.ds(0, layers - own)], small_recv.at[1]
    ).wait()
    for i in range(per // 2):
        rows_of = jnp.concatenate(
            [
                jnp.zeros((BLK, 128), jnp.float32),
                ball[:, i, :],
                jnp.zeros((BLK - layers, 128), jnp.float32),
            ],
            axis=0,
        )
        btr[2 * i : 2 * i + 2] = rows_of.T.astype(jnp.bfloat16).reshape(2, BLK, 128)
    done = ring_until(done, 2 * SKEW)
    table_load.wait()
    for load in loads:
        load.wait()

    low_lanes = lax.broadcasted_iota(jnp.int32, (BLK, 128), 1) < BLK
    batch = owners // 4

    def one_layer(layer, now, done):
        act, after = (act_even, act_odd)[now], (act_odd, act_even)[now]
        recv = (recv_even, recv_odd)[now]
        home, base = layer // own, lax.rem(layer, own) * 4
        begin = jnp.maximum(done, needed(layer))
        steps = jnp.maximum(needed(jnp.minimum(layer + 1, layers - 1)) - begin, 0)

        def feed(done, portion):
            return ring_until(done, begin + steps * portion // 8)


        @pl.when(layer >= 2)
        def _():
            sent = send.at[now, pl.ds(0, owners - 1)]
            pltpu.make_async_copy(sent, sent, a2a_send.at[now]).wait()

        def pair(q):
            first = tabs[home, base, q]
            second = tabs[home, base, owners + q]
            return jnp.where(low_lanes, act[first], act[second])

        def give(d, c):
            q = lax.rem(me + d, owners)
            send[now, q] = pair(q)
            pltpu.make_async_remote_copy(
                src_ref=send.at[now, q], dst_ref=recv.at[me],
                send_sem=a2a_send.at[now], recv_sem=a2a_recv.at[now, d // batch],
                device_id={"neuron": q}, device_id_type=MESH,
            ).start()
            return c

        lax.fori_loop(1, owners // 2, give, 0)

        done = ring_until(done, jnp.where(layer > 0, begin + steps // 8, 0))
        lax.fori_loop(owners // 2, owners, give, 0)
        recv[me] = pair(me)

        done = ring_until(done, needed(layer))
        done = feed(done, 2)
        pick = jnp.where(
            lax.broadcasted_iota(jnp.int32, (BLK, 128), 0) == layer, 1.0, 0.0
        ).astype(jnp.bfloat16)

        def near_group(g, c):
            joined, packed = [], []
            for i in range(GROUP):
                j = g * GROUP + i
                near = [act[tabs[home, base + 1, 3 * j + k]] for k in range(3)]
                joined.append(jnp.concatenate(near + [pick], axis=0))
                w = wbuf[layer, j]
                packed.append(
                    jnp.concatenate(
                        [w[:, :128], jnp.where(low_lanes, w[:, 128:], btr[j])], axis=1
                    )
                )
            sums = [
                jnp.dot(p, x, preferred_element_type=jnp.float32) for p, x in zip(packed, joined)
            ]
            for i in range(GROUP):
                total[g * GROUP + i] = sums[i]
            return c

        groups = per // GROUP

        lax.fori_loop(0, groups // 2, near_group, 0)
        done = feed(done, 3)
        lax.fori_loop(groups // 2, groups, near_group, 0)
        for i in range(4):
            done = feed(done, 4 + i)
            got = recv.at[pl.ds(0, batch - 1 if i == 0 else batch)]
            pltpu.make_async_copy(got, got, a2a_recv.at[now, i]).wait()

        def far_group(g, c):
            pairs, straights, sums, done = [], [], [], []
            for i in range(GROUP):
                j = g * GROUP + i
                pairs.append(recv[tabs[home, base + 2, j]])
                slot = jnp.zeros((BLK, 128), jnp.int32) + tabs[home, base + 2, per + j]
                straights.append(low_lanes == (slot == 0))
            for i in range(GROUP):
                joined = jnp.concatenate([jnp.zeros((BLK, 128), jnp.bfloat16), pairs[i]], axis=0)
                w = wbuf[layer, g * GROUP + i][:, 128:]
                sums.append(jnp.dot(w, joined, preferred_element_type=jnp.float32))
            for i in range(GROUP):
                far = jnp.where(straights[i], sums[i], pltpu.roll(sums[i], BLK, 1))
                z = total[g * GROUP + i] + far
                done.append(jnp.minimum(jnp.maximum(z, 0.0), 32.0).astype(jnp.bfloat16))
            for i in range(GROUP):
                after[g * GROUP + i] = done[i]
            return c

        lax.fori_loop(0, groups // 2, far_group, 0)
        done = feed(done, 8)
        lax.fori_loop(groups // 2, groups, far_group, 0)
        return done

    def two_layers(i, done):
        done = one_layer(2 * i, 0, done)
        return one_layer(2 * i + 1, 1, done)

    done = lax.fori_loop(0, layers // 2, two_layers, done)
    ring_until(done, end)
    o_ref[...] = act_even[...]

    for par in range(2):
        sent = send.at[par, pl.ds(0, owners - 1)]
        pltpu.make_async_copy(sent, sent, a2a_send.at[par]).wait()

    for side in (0, 1):
        for t in range(own):
            count = (first, second)[t][side] * UNIT
            sent = wbuf.at[pl.ds(0, last), pl.ds(0, count)]
            pltpu.make_async_copy(sent, sent, ring_send.at[side, t]).wait()
    out = tall.at[pl.ds(0, sections - 1)]
    pltpu.make_async_copy(out, out, small_send.at[0]).wait()
    out = ball.at[pl.ds(0, layers - own)]
    pltpu.make_async_copy(out, out, small_send.at[1]).wait()


def local(samples, weights, biases, near_blocks, remote_cols):
    batches, rows, width = samples.shape
    sections = lax.axis_size("segment")
    owners = lax.axis_size("neuron")
    s = lax.axis_index("segment")
    me = lax.axis_index("neuron")
    per = width // BLK
    own = weights.shape[0]
    layers = own * sections
    share = rows // sections
    count = batches * share
    mine = lax.dynamic_slice_in_dim(samples, s * share, share, 1).reshape(count, width)
    x = mine.T
    x = jnp.concatenate([x, x], axis=1).reshape(per, BLK, 128)
    table = tables(remote_cols, near_blocks, owners, me)
    bias = biases.astype(jnp.float32).reshape(own, width // 128, 128)
    dims = (sections, owners, per, layers, count)
    bf16, f32 = jnp.bfloat16, jnp.float32
    out = pl.pallas_call(
        functools.partial(kernel, dims),
        out_shape=jax.ShapeDtypeStruct((per, BLK, 128), bf16),
        in_specs=[
            pl.BlockSpec(memory_space=pl.ANY),
            pl.BlockSpec(memory_space=pl.ANY),
            pl.BlockSpec(memory_space=pltpu.VMEM),
            pl.BlockSpec(memory_space=pltpu.VMEM),
        ],
        out_specs=pl.BlockSpec(memory_space=pltpu.VMEM),
        scratch_shapes=[
            pltpu.VMEM((per, BLK, 128), bf16),
            pltpu.VMEM((per, BLK, 128), bf16),
            pltpu.VMEM((per, BLK, 128), f32),
            pltpu.VMEM((2, owners, BLK, 128), bf16),
            pltpu.VMEM((owners, BLK, 128), bf16),
            pltpu.VMEM((owners, BLK, 128), bf16),
            pltpu.VMEM((layers, per, BLK, 256), bf16),
            pltpu.VMEM((layers, width // 128, 128), f32),
            pltpu.VMEM((per, BLK, 128), bf16),
            pltpu.VMEM((sections, own * 4, 128), jnp.int32),
            pltpu.SMEM((sections, own * 4, 128), jnp.int32),
            pltpu.SemaphoreType.DMA((3,)),
            pltpu.SemaphoreType.DMA((2,)),
            pltpu.SemaphoreType.DMA((2,)),
            pltpu.SemaphoreType.DMA((2,)),
            pltpu.SemaphoreType.DMA((2, 4)),
            pltpu.SemaphoreType.DMA((2, own)),
            pltpu.SemaphoreType.DMA((2, sections, own * per // UNIT)),
        ],
        compiler_params=pltpu.CompilerParams(
            collective_id=0, has_side_effects=True, vmem_limit_bytes=48 * 1024 * 1024
        ),
    )(x, weights.reshape(own, per, BLK, 256), bias, table)
    y = out.reshape(width, 128)[:, :count].T
    return y.reshape(batches, share, width)


def solution(mesh):
    return jax.shard_map(
        local,
        mesh=mesh,
        in_specs=(
            P(None, None, "neuron"),
            P("segment", "neuron", None),
            P("segment", "neuron"),
            P("segment", "neuron", None),
            P("segment", None),
        ),
        out_specs=P(None, "segment", "neuron"),
        check_vma=False,
    )
```

```python
import functools
import math

import jax
import jax.numpy as jnp
from jax import lax
from jax.experimental import pallas as pl
from jax.experimental.pallas import tpu as pltpu
from jax.sharding import PartitionSpec as P

MESH = pl.DeviceIdType.MESH
BLK = 64
UNIT = 2
FIRST_SHARE = 8
SECOND_SHARE = 7
SKEW = 3
LEAD = 31
BEHIND = 5
GROUP = 16


def tables(cols, near, owners, me):
    layers = cols.shape[0]
    grid = cols.reshape(layers, owners, -1)
    per = grid.shape[2]
    place = lax.broadcasted_iota(jnp.int32, grid.shape, 2)
    asked = (grid // per) == me
    first = jnp.min(jnp.where(asked, place, per - 1), axis=2, keepdims=True)
    last = jnp.max(jnp.where(asked, place, 0), axis=2, keepdims=True)
    inside = grid % per
    send = jnp.concatenate(
        [
            jnp.sum(jnp.where(place == first, inside, 0), axis=2),
            jnp.sum(jnp.where(place == last, inside, 0), axis=2),
        ],
        axis=1,
    )
    mine = lax.dynamic_index_in_dim(grid, me, 1, keepdims=False) // per
    same = mine[:, :, None] == mine[:, None, :]
    earlier = lax.broadcasted_iota(jnp.int32, same.shape, 2) < lax.broadcasted_iota(
        jnp.int32, same.shape, 1
    )
    slot = jnp.max(jnp.where(same & earlier, 1, 0), axis=2)
    row = lambda v: jnp.pad(v, ((0, 0), (0, 128 - v.shape[1])))
    far = jnp.concatenate([mine, slot], axis=1)
    packed = jnp.stack(
        [row(send), row(near.reshape(layers, -1)), row(far), jnp.zeros((layers, 128), jnp.int32)],
        axis=1,
    )
    return packed.reshape(layers * 4, 128)


def kernel(
    dims, x_ref, w_ref, b_ref, t_ref, o_ref,
    act_even, act_odd, total, send, recv_even, recv_odd, wbuf, ball, btr, tall, tabs,
    local_sem, small_send, small_recv, a2a_send, a2a_recv, ring_send, ring_recv,
):
    sections, owners, per, layers, rows = dims
    own = layers // sections
    s = lax.axis_index("segment")
    me = lax.axis_index("neuron")
    ahead = lax.rem(s + 1, sections)
    behind = lax.rem(s + sections - 1, sections)
    last = sections - 1

    loads = [
        pltpu.make_async_copy(x_ref, act_even, local_sem.at[0]),
        pltpu.make_async_copy(w_ref, wbuf.at[pl.ds(s * own, own)], local_sem.at[1]),
    ]
    for load in loads:
        load.start()
    tall[pl.ds(s, 1)] = t_ref[...][None]
    ball[pl.ds(s * own, own)] = b_ref[...]

    barrier = pltpu.get_barrier_semaphore()

    def greet(d, carry):
        pl.semaphore_signal(
            barrier, inc=1, device_id={"neuron": lax.rem(me + d, owners)}, device_id_type=MESH
        )
        return carry

    lax.fori_loop(1, owners, greet, 0)

    def greet_section(d, carry):
        pl.semaphore_signal(
            barrier, inc=1, device_id={"segment": lax.rem(s + d, sections)}, device_id_type=MESH
        )
        return carry

    lax.fori_loop(1, sections, greet_section, 0)
    pl.semaphore_wait(barrier, owners - 1 + sections - 1)

    def share(d, carry):
        to = {"segment": lax.rem(s + d, sections)}
        pltpu.make_async_remote_copy(
            src_ref=tall.at[pl.ds(s, 1)], dst_ref=tall.at[pl.ds(s, 1)],
            send_sem=small_send.at[0], recv_sem=small_recv.at[0],
            device_id=to, device_id_type=MESH,
        ).start()
        pltpu.make_async_remote_copy(
            src_ref=ball.at[pl.ds(s * own, own)], dst_ref=ball.at[pl.ds(s * own, own)],
            send_sem=small_send.at[1], recv_sem=small_recv.at[1],
            device_id=to, device_id_type=MESH,
        ).start()
        return carry

    lax.fori_loop(1, sections, share, 0)

    units = per // UNIT
    first = (FIRST_SHARE, units - FIRST_SHARE)
    second = (SECOND_SHARE, units - SECOND_SHARE)
    window = (first[0] + second[0], first[1] + second[1])
    lone = window[0] - SKEW
    end = window[1] * sections

    def ring(source, home, i, side, to, own_source):
        later = (i >= first[side]).astype(jnp.int32)
        begin = 0 if side == 0 else first[0] + later * (second[0] - first[0])
        place = begin + i - later * first[side]
        at = pl.ds(place * UNIT, UNIT)
        layer = home * own + later
        return pltpu.make_async_remote_copy(
            src_ref=source.at[later if own_source else layer, at], dst_ref=wbuf.at[layer, at],
            send_sem=ring_send.at[side, later], recv_sem=ring_recv.at[side, home, i],
            device_id={"segment": to}, device_id_type=MESH,
        )

    def hand_on(side, home, i, fine, hops):
        home, i = jnp.clip(home, 0, last), jnp.clip(i, 0, window[side] - 1)
        copy = ring(wbuf, home, i, side, (ahead, behind)[side], False)

        @pl.when(fine)
        def _():
            copy.wait_recv()

        @pl.when(fine & (hops < last))
        def _():
            copy.start()

    own_base = jnp.where(s == last, SKEW * (last - 1), window[0] * s)
    own_early = jnp.where(s == 0, window[1], jnp.minimum(window[1], SKEW * (sections - s)))
    own_late = window[1] * (s - 1) + SKEW * (sections - s) - own_early

    def give_own(side, i, fine):
        @pl.when(fine)
        def _():
            i_in = jnp.clip(i, 0, window[side] - 1)
            ring(w_ref, s, i_in, side, (ahead, behind)[side], True).start()

    def ring_step(e):
        t = e - own_base
        give_own(0, jnp.where(e < SKEW, e, t), (e < SKEW) | ((t >= SKEW) & (t < window[0])))
        t = e - own_late
        give_own(
            1,
            jnp.where(e < own_early, e, t),
            (e < own_early) | ((s > 0) & (t >= own_early) & (t < window[1])),
        )

        inner = (e >= SKEW) & (e < SKEW * s)
        home = jnp.where(inner, s - e // SKEW, -1)
        i = lax.rem(e, SKEW)
        t = e - SKEW * s
        fits = (s >= 1) & (t >= 0) & (t < window[0])
        home, i = jnp.where(fits, 0, home), jnp.where(fits, t, i)
        t = t - window[0]
        fits = (t >= 0) & (t < lone * (s - 1))
        t = jnp.maximum(t, 0)
        home = jnp.where(fits, 1 + t // lone, home)
        i = jnp.where(fits, SKEW + lax.rem(t, lone), i)
        t = e - window[0] * (s + 1)
        fits = (t >= 0) & (t < SKEW * (last - 1 - s))
        t_in = jnp.maximum(t, 0)
        home = jnp.where(fits, last - 1 - t_in // SKEW, home)
        i = jnp.where(fits, lax.rem(t_in, SKEW), i)
        t = t - SKEW * (last - 1 - s)
        fits = (s < last) & (t >= 0) & (t < window[0])
        home, i = jnp.where(fits, last, home), jnp.where(fits, t, i)
        hand_on(0, home, i, home >= 0, lax.rem(s - home + sections, sections))

        t = e - SKEW * (sections + 1 + s)
        t_in = jnp.maximum(t, 0)
        home = t_in // lone
        fine = (t >= 0) & (home > s) & (home < last)
        hand_on(0, home, SKEW + lax.rem(t_in, lone), fine, s - home + sections)

        for t, low, high, hops in (
            (e - SKEW * (sections - s), 0, s, sections - s),
            (e + SKEW * s, s + 1, sections, -s),
        ):
            t_in = jnp.maximum(t, 0)
            home = t_in // window[1]
            fine = (t >= 0) & (home >= low) & (home < high)
            hand_on(1, home, lax.rem(t_in, window[1]), fine, home + hops)

    def ring_until(low, high):
        def one(e, carry):
            ring_step(e)
            return carry

        lax.fori_loop(low, high, one, 0)
        return jnp.maximum(low, high)

    def needed(layer):
        return jnp.minimum(LEAD + layer * (end + BEHIND - LEAD) // (layers - 1), end)

    done = ring_until(0, SKEW)
    pltpu.make_async_copy(
        tall.at[pl.ds(0, sections - 1)], tall.at[pl.ds(0, sections - 1)], small_recv.at[0]
    ).wait()
    table_load = pltpu.make_async_copy(tall, tabs, local_sem.at[2])
    table_load.start()
    pltpu.make_async_copy(
        ball.at[pl.ds(0, layers - own)], ball.at[pl.ds(0, layers - own)], small_recv.at[1]
    ).wait()
    for i in range(per // 2):
        rows_of = jnp.concatenate(
            [
                jnp.zeros((BLK, 128), jnp.float32),
                ball[:, i, :],
                jnp.zeros((BLK - layers, 128), jnp.float32),
            ],
            axis=0,
        )
        btr[2 * i : 2 * i + 2] = rows_of.T.astype(jnp.bfloat16).reshape(2, BLK, 128)
    done = ring_until(done, 2 * SKEW)
    table_load.wait()
    for load in loads:
        load.wait()

    low_lanes = lax.broadcasted_iota(jnp.int32, (BLK, 128), 1) < BLK
    batch = owners // 4
    chips, chip = owners // 2, me // 2
    side = math.isqrt(chips)

    def distance(offset):
        return sum(min(d, side - d) for d in divmod(offset, side))

    ranked = sorted(range(1, chips), key=lambda o: (-distance(o), o % side == 0 or o < side))
    order = []
    for begin in range(0, chips - 1, 5):
        taken = ranked[begin : begin + 5]
        order.append((begin, len(taken), sum(o * chips**i for i, o in enumerate(taken))))

    def one_layer(layer, now, done):
        act, after = (act_even, act_odd)[now], (act_odd, act_even)[now]
        recv = (recv_even, recv_odd)[now]
        home, base = layer // own, lax.rem(layer, own) * 4
        begin = jnp.maximum(done, needed(layer))
        steps = jnp.maximum(needed(jnp.minimum(layer + 1, layers - 1)) - begin, 0)

        def feed(done, portion):
            return ring_until(done, begin + steps * portion // 8)


        @pl.when(layer >= 2)
        def _():
            sent = send.at[now, pl.ds(0, owners - 1)]
            pltpu.make_async_copy(sent, sent, a2a_send.at[now]).wait()

        def pair(q):
            first = tabs[home, base, q]
            second = tabs[home, base, owners + q]
            return jnp.where(low_lanes, act[first], act[second])

        def give(q, number):
            send[now, q] = pair(q)
            pltpu.make_async_remote_copy(
                src_ref=send.at[now, q], dst_ref=recv.at[me],
                send_sem=a2a_send.at[now], recv_sem=a2a_recv.at[now, number // batch],
                device_id={"neuron": q}, device_id_type=MESH,
            ).start()

        def give_chip(number, packed):
            offset, packed = lax.rem(packed, chips), packed // chips
            x = lax.rem(chip // side + offset // side, side)
            y = lax.rem(chip + offset, side)
            for core in range(2):
                q = (x * side + y) * 2 + lax.rem(me + core, 2)
                give(q, number * 2 + core)
            return packed

        for begin, many, packed in order:
            lax.fori_loop(begin, begin + many, give_chip, jnp.int32(packed))
        give(me + 1 - 2 * lax.rem(me, 2), owners - 2)
        recv[me] = pair(me)

        done = ring_until(done, needed(layer))
        done = feed(done, 2)
        pick = jnp.where(
            lax.broadcasted_iota(jnp.int32, (BLK, 128), 0) == layer, 1.0, 0.0
        ).astype(jnp.bfloat16)

        def near_group(g, c):
            joined, packed = [], []
            for i in range(GROUP):
                j = g * GROUP + i
                near = [act[tabs[home, base + 1, 3 * j + k]] for k in range(3)]
                joined.append(jnp.concatenate(near + [pick], axis=0))
                w = wbuf[layer, j]
                packed.append(
                    jnp.concatenate(
                        [w[:, :128], jnp.where(low_lanes, w[:, 128:], btr[j])], axis=1
                    )
                )
            sums = [
                jnp.dot(p, x, preferred_element_type=jnp.float32) for p, x in zip(packed, joined)
            ]
            for i in range(GROUP):
                total[g * GROUP + i] = sums[i]
            return c

        groups = per // GROUP

        lax.fori_loop(0, groups // 2, near_group, 0)
        done = feed(done, 3)
        lax.fori_loop(groups // 2, groups, near_group, 0)
        for i in range(4):
            done = feed(done, 4 + i)
            got = recv.at[pl.ds(0, batch - 1 if i == 3 else batch)]
            pltpu.make_async_copy(got, got, a2a_recv.at[now, i]).wait()

        def far_group(g, c):
            pairs, straights, sums, done = [], [], [], []
            for i in range(GROUP):
                j = g * GROUP + i
                pairs.append(recv[tabs[home, base + 2, j]])
                slot = jnp.zeros((BLK, 128), jnp.int32) + tabs[home, base + 2, per + j]
                straights.append(low_lanes == (slot == 0))
            for i in range(GROUP):
                joined = jnp.concatenate([jnp.zeros((BLK, 128), jnp.bfloat16), pairs[i]], axis=0)
                w = wbuf[layer, g * GROUP + i][:, 128:]
                sums.append(jnp.dot(w, joined, preferred_element_type=jnp.float32))
            for i in range(GROUP):
                far = jnp.where(straights[i], sums[i], pltpu.roll(sums[i], BLK, 1))
                z = total[g * GROUP + i] + far
                done.append(jnp.minimum(jnp.maximum(z, 0.0), 32.0).astype(jnp.bfloat16))
            for i in range(GROUP):
                after[g * GROUP + i] = done[i]
            return c

        lax.fori_loop(0, groups // 2, far_group, 0)
        done = feed(done, 8)
        lax.fori_loop(groups // 2, groups, far_group, 0)
        return done

    def two_layers(i, done):
        done = one_layer(2 * i, 0, done)
        return one_layer(2 * i + 1, 1, done)

    done = lax.fori_loop(0, layers // 2, two_layers, done)
    ring_until(done, end)
    o_ref[...] = act_even[...]

    for par in range(2):
        sent = send.at[par, pl.ds(0, owners - 1)]
        pltpu.make_async_copy(sent, sent, a2a_send.at[par]).wait()

    for side in (0, 1):
        for t in range(own):
            count = (first, second)[t][side] * UNIT
            sent = wbuf.at[pl.ds(0, last), pl.ds(0, count)]
            pltpu.make_async_copy(sent, sent, ring_send.at[side, t]).wait()
    out = tall.at[pl.ds(0, sections - 1)]
    pltpu.make_async_copy(out, out, small_send.at[0]).wait()
    out = ball.at[pl.ds(0, layers - own)]
    pltpu.make_async_copy(out, out, small_send.at[1]).wait()


def local(samples, weights, biases, near_blocks, remote_cols):
    batches, rows, width = samples.shape
    sections = lax.axis_size("segment")
    owners = lax.axis_size("neuron")
    s = lax.axis_index("segment")
    me = lax.axis_index("neuron")
    per = width // BLK
    own = weights.shape[0]
    layers = own * sections
    share = rows // sections
    count = batches * share
    mine = lax.dynamic_slice_in_dim(samples, s * share, share, 1).reshape(count, width)
    x = mine.T
    x = jnp.concatenate([x, x], axis=1).reshape(per, BLK, 128)
    table = tables(remote_cols, near_blocks, owners, me)
    bias = biases.astype(jnp.float32).reshape(own, width // 128, 128)
    dims = (sections, owners, per, layers, count)
    bf16, f32 = jnp.bfloat16, jnp.float32
    out = pl.pallas_call(
        functools.partial(kernel, dims),
        out_shape=jax.ShapeDtypeStruct((per, BLK, 128), bf16),
        in_specs=[
            pl.BlockSpec(memory_space=pl.ANY),
            pl.BlockSpec(memory_space=pl.ANY),
            pl.BlockSpec(memory_space=pltpu.VMEM),
            pl.BlockSpec(memory_space=pltpu.VMEM),
        ],
        out_specs=pl.BlockSpec(memory_space=pltpu.VMEM),
        scratch_shapes=[
            pltpu.VMEM((per, BLK, 128), bf16),
            pltpu.VMEM((per, BLK, 128), bf16),
            pltpu.VMEM((per, BLK, 128), f32),
            pltpu.VMEM((2, owners, BLK, 128), bf16),
            pltpu.VMEM((owners, BLK, 128), bf16),
            pltpu.VMEM((owners, BLK, 128), bf16),
            pltpu.VMEM((layers, per, BLK, 256), bf16),
            pltpu.VMEM((layers, width // 128, 128), f32),
            pltpu.VMEM((per, BLK, 128), bf16),
            pltpu.VMEM((sections, own * 4, 128), jnp.int32),
            pltpu.SMEM((sections, own * 4, 128), jnp.int32),
            pltpu.SemaphoreType.DMA((3,)),
            pltpu.SemaphoreType.DMA((2,)),
            pltpu.SemaphoreType.DMA((2,)),
            pltpu.SemaphoreType.DMA((2,)),
            pltpu.SemaphoreType.DMA((2, 4)),
            pltpu.SemaphoreType.DMA((2, own)),
            pltpu.SemaphoreType.DMA((2, sections, own * per // UNIT)),
        ],
        compiler_params=pltpu.CompilerParams(
            collective_id=0, has_side_effects=True, vmem_limit_bytes=48 * 1024 * 1024
        ),
    )(x, weights.reshape(own, per, BLK, 256), bias, table)
    y = out.reshape(width, 128)[:, :count].T
    return y.reshape(batches, share, width)


def solution(mesh):
    return jax.shard_map(
        local,
        mesh=mesh,
        in_specs=(
            P(None, None, "neuron"),
            P("segment", "neuron", None),
            P("segment", "neuron"),
            P("segment", "neuron", None),
            P("segment", None),
        ),
        out_specs=P(None, "segment", "neuron"),
        check_vma=False,
    )
```

```python
import functools
import math

import jax
import jax.numpy as jnp
from jax import lax
from jax.experimental import pallas as pl
from jax.experimental.pallas import tpu as pltpu
from jax.sharding import PartitionSpec as P

MESH = pl.DeviceIdType.MESH
BLK = 64
UNIT = 2
FIRST_SHARE = 8
SECOND_SHARE = 7
SKEW = 3
LEAD = 31
BEHIND = 5
GROUP = 16


def table(cols, per, me, roll):
    rows = cols.shape[0]
    many = 128 // per
    lane = lax.broadcasted_iota(jnp.int32, (rows, 128), 1)
    row = lax.broadcasted_iota(jnp.int32, (rows, 128), 0)
    key = lax.rem(lane, per) * per + lax.rem(cols, per)
    asked = cols // per == me
    result = jnp.zeros((rows, 128), jnp.int32)
    for g in range(many):
        here = asked & (lane // per == g)
        low = jnp.min(jnp.where(here, key, per * per - 1), axis=1, keepdims=True)
        high = jnp.max(jnp.where(here, key, 0), axis=1, keepdims=True)
        result = jnp.where(lane == g, lax.rem(low, per), result)
        result = jnp.where(lane == many + g, lax.rem(high, per), result)
    mine = jnp.sum(jnp.where(row == me // many, cols // per, 0), axis=0, keepdims=True)
    mine = jnp.zeros((rows, 128), jnp.int32) + mine
    mine = roll(mine, lax.rem(per - per * lax.rem(me, many) + 128, 128))
    slot = jnp.zeros((rows, 128), jnp.int32)
    for k in range(1, per):
        slot = jnp.where((roll(mine, k) == mine) & (lane >= per + k), 1, slot)
    far = (lane >= per) & (lane < 2 * per)
    result = jnp.where(far & (row == 3), mine, result)
    return jnp.where(far & (row == 4), slot, result)


def kernel(
    dims, x_ref, w_ref, b_ref, near_ref, cols_ref, o_ref,
    x_in,
    act_even, act_odd, total, send, recv_even, recv_odd, wbuf, ball, btr, tall, tabs,
    local_sem, small_send, small_recv, a2a_send, a2a_recv, ring_send, ring_recv,
):
    sections, owners, per, layers, rows = dims
    own = layers // sections
    s = lax.axis_index("segment")
    me = lax.axis_index("neuron")
    ahead = lax.rem(s + 1, sections)
    behind = lax.rem(s + sections - 1, sections)
    last = sections - 1

    barrier = pltpu.get_barrier_semaphore()

    def greet(d, carry):
        pl.semaphore_signal(
            barrier, inc=1, device_id={"neuron": lax.rem(me + d, owners)}, device_id_type=MESH
        )
        return carry

    lax.fori_loop(1, owners, greet, 0)

    def greet_section(d, carry):
        pl.semaphore_signal(
            barrier, inc=1, device_id={"segment": lax.rem(s + d, sections)}, device_id_type=MESH
        )
        return carry

    lax.fori_loop(1, sections, greet_section, 0)

    share_rows = rows // x_in.shape[0]
    mine = x_ref.at[:, pl.ds(pl.multiple_of(s * share_rows, share_rows), share_rows)]
    loads = [
        pltpu.make_async_copy(mine, x_in, local_sem.at[0]),
        pltpu.make_async_copy(w_ref, wbuf.at[pl.ds(s * own, own)], local_sem.at[1]),
    ]
    for load in loads:
        load.start()
    pl.semaphore_wait(barrier, owners - 1 + sections - 1)

    units = per // UNIT
    first = (FIRST_SHARE, units - FIRST_SHARE)
    second = (SECOND_SHARE, units - SECOND_SHARE)
    window = (first[0] + second[0], first[1] + second[1])
    lone = window[0] - SKEW
    end = window[1] * sections

    def ring(home, i, side):
        later = (i >= first[side]).astype(jnp.int32)
        begin = 0 if side == 0 else first[0] + later * (second[0] - first[0])
        place = begin + i - later * first[side]
        at = pl.ds(place * UNIT, UNIT)
        layer = home * own + later
        return pltpu.make_async_remote_copy(
            src_ref=wbuf.at[layer, at], dst_ref=wbuf.at[layer, at],
            send_sem=ring_send.at[side, later], recv_sem=ring_recv.at[side, home, i],
            device_id={"segment": (ahead, behind)[side]}, device_id_type=MESH,
        )

    def hand_on(side, home, i, fine, hops):
        home, i = jnp.clip(home, 0, last), jnp.clip(i, 0, window[side] - 1)
        copy = ring(home, i, side)

        @pl.when(fine)
        def _():
            copy.wait_recv()

        @pl.when(fine & (hops < last))
        def _():
            copy.start()

    own_base = jnp.where(s == last, SKEW * (last - 1), window[0] * s)
    own_early = jnp.where(s == 0, window[1], jnp.minimum(window[1], SKEW * (sections - s)))
    own_late = window[1] * (s - 1) + SKEW * (sections - s) - own_early

    def give_own(side, i, fine):
        @pl.when(fine)
        def _():
            i_in = jnp.clip(i, 0, window[side] - 1)
            ring(s, i_in, side).start()

    def ring_step(e):
        t = e - own_base
        give_own(0, jnp.where(e < SKEW, e, t), (e < SKEW) | ((t >= SKEW) & (t < window[0])))
        t = e - own_late
        give_own(
            1,
            jnp.where(e < own_early, e, t),
            (e < own_early) | ((s > 0) & (t >= own_early) & (t < window[1])),
        )

        inner = (e >= SKEW) & (e < SKEW * s)
        home = jnp.where(inner, s - e // SKEW, -1)
        i = lax.rem(e, SKEW)
        t = e - SKEW * s
        fits = (s >= 1) & (t >= 0) & (t < window[0])
        home, i = jnp.where(fits, 0, home), jnp.where(fits, t, i)
        t = t - window[0]
        fits = (t >= 0) & (t < lone * (s - 1))
        t = jnp.maximum(t, 0)
        home = jnp.where(fits, 1 + t // lone, home)
        i = jnp.where(fits, SKEW + lax.rem(t, lone), i)
        t = e - window[0] * (s + 1)
        fits = (t >= 0) & (t < SKEW * (last - 1 - s))
        t_in = jnp.maximum(t, 0)
        home = jnp.where(fits, last - 1 - t_in // SKEW, home)
        i = jnp.where(fits, lax.rem(t_in, SKEW), i)
        t = t - SKEW * (last - 1 - s)
        fits = (s < last) & (t >= 0) & (t < window[0])
        home, i = jnp.where(fits, last, home), jnp.where(fits, t, i)
        hand_on(0, home, i, home >= 0, lax.rem(s - home + sections, sections))

        t = e - SKEW * (sections + 1 + s)
        t_in = jnp.maximum(t, 0)
        home = t_in // lone
        fine = (t >= 0) & (home > s) & (home < last)
        hand_on(0, home, SKEW + lax.rem(t_in, lone), fine, s - home + sections)

        for t, low, high, hops in (
            (e - SKEW * (sections - s), 0, s, sections - s),
            (e + SKEW * s, s + 1, sections, -s),
        ):
            t_in = jnp.maximum(t, 0)
            home = t_in // window[1]
            fine = (t >= 0) & (home >= low) & (home < high)
            hand_on(1, home, lax.rem(t_in, window[1]), fine, home + hops)

    def ring_until(low, high):
        def one(e, carry):
            ring_step(e)
            return carry

        lax.fori_loop(low, high, one, 0)
        return jnp.maximum(low, high)

    def needed(layer):
        return jnp.minimum(LEAD + layer * (end + BEHIND - LEAD) // (layers - 1), end)

    def own_table(t):
        cols = jnp.concatenate(
            [cols_ref[t : t + 1, r : r + 128] for r in range(0, cols_ref.shape[1], 128)], axis=0
        )
        tall[s * own + t] = table(cols, per, me, lambda v, k: pltpu.roll(v, k, 1))
        for k in range(3):
            tall[s * own + t, k : k + 1, per : 2 * per] = near_ref[k, t : t + 1, :]
        for i in range(per // 2):
            ball[s * own + t, i : i + 1, :] = b_ref[t : t + 1, i * 128 : (i + 1) * 128].astype(
                jnp.float32
            )

    def share(d, carry):
        to = {"segment": lax.rem(s + d, sections)}
        pltpu.make_async_remote_copy(
            src_ref=tall.at[pl.ds(s * own, own)], dst_ref=tall.at[pl.ds(s * own, own)],
            send_sem=small_send.at[0], recv_sem=small_recv.at[0],
            device_id=to, device_id_type=MESH,
        ).start()
        pltpu.make_async_remote_copy(
            src_ref=ball.at[pl.ds(s * own, own)], dst_ref=ball.at[pl.ds(s * own, own)],
            send_sem=small_send.at[1], recv_sem=small_recv.at[1],
            device_id=to, device_id_type=MESH,
        ).start()
        return carry


    def bias_columns(i):
        rows_of = jnp.concatenate(
            [
                jnp.zeros((BLK, 128), jnp.float32),
                ball[:, i, :],
                jnp.zeros((BLK - layers, 128), jnp.float32),
            ],
            axis=0,
        )
        btr[2 * i : 2 * i + 2] = rows_of.T.astype(jnp.bfloat16).reshape(2, BLK, 128)

    def take_samples(i):
        part = x_in[:, :, i * 128 : (i + 1) * 128].reshape(rows, 128).astype(jnp.float32)
        part = jnp.concatenate([part, part], axis=0).T.astype(jnp.bfloat16)
        act_even[2 * i : 2 * i + 2] = part.reshape(2, BLK, 128)

    loads[1].wait()
    done = ring_until(0, SKEW)
    for t in range(own):
        own_table(t)
        done = ring_until(done, done + 1)
    lax.fori_loop(1, sections, share, 0)
    loads[0].wait()
    for i in range(per // 2):
        take_samples(i)
        if i % 4 == 3:
            done = ring_until(done, done + 1)
    pltpu.make_async_copy(
        tall.at[pl.ds(0, layers - own)], tall.at[pl.ds(0, layers - own)], small_recv.at[0]
    ).wait()
    table_load = pltpu.make_async_copy(tall, tabs, local_sem.at[2])
    table_load.start()
    pltpu.make_async_copy(
        ball.at[pl.ds(0, layers - own)], ball.at[pl.ds(0, layers - own)], small_recv.at[1]
    ).wait()
    for i in range(per // 2):
        bias_columns(i)
        if i % 4 == 3:
            done = ring_until(done, done + 1)
    table_load.wait()

    low_lanes = lax.broadcasted_iota(jnp.int32, (BLK, 128), 1) < BLK
    batch = owners // 4
    many = 128 // per
    chips, chip = owners // 2, me // 2
    side = math.isqrt(chips)

    def distance(offset):
        return sum(min(d, side - d) for d in divmod(offset, side))

    ranked = sorted(range(1, chips), key=lambda o: (-distance(o), o % side == 0 or o < side))
    order = []
    for begin in range(0, chips - 1, 5):
        taken = ranked[begin : begin + 5]
        order.append((begin, len(taken), sum(o * chips**i for i, o in enumerate(taken))))

    def one_layer(layer, now, done):
        act, after = (act_even, act_odd)[now], (act_odd, act_even)[now]
        recv = (recv_even, recv_odd)[now]
        begin = begin_steps = jnp.maximum(done, needed(layer))
        steps = jnp.maximum(needed(jnp.minimum(layer + 1, layers - 1)) - begin, 0)

        def feed(done, portion):
            return ring_until(done, begin + steps * portion // 8)


        @pl.when(layer >= 2)
        def _():
            sent = send.at[now, pl.ds(0, owners - 1)]
            pltpu.make_async_copy(sent, sent, a2a_send.at[now]).wait()

        def pair(q):
            first = tabs[layer, q // many, lax.rem(q, many)]
            second = tabs[layer, q // many, many + lax.rem(q, many)]
            return jnp.where(low_lanes, act[first], act[second])

        def give(q, number):
            send[now, q] = pair(q)
            pltpu.make_async_remote_copy(
                src_ref=send.at[now, q], dst_ref=recv.at[me],
                send_sem=a2a_send.at[now], recv_sem=a2a_recv.at[now, number // batch],
                device_id={"neuron": q}, device_id_type=MESH,
            ).start()

        def give_chip(number, packed):
            offset, packed = lax.rem(packed, chips), packed // chips
            x = lax.rem(chip // side + offset // side, side)
            y = lax.rem(chip + offset, side)
            for core in range(2):
                q = (x * side + y) * 2 + lax.rem(me + core, 2)
                give(q, number * 2 + core)
            return packed

        for place, amount, packed in order:
            lax.fori_loop(place, place + amount, give_chip, jnp.int32(packed))
            if place == 5:
                done = ring_until(done, jnp.where(layer > 0, begin_steps + steps // 8, 0))
        give(me + 1 - 2 * lax.rem(me, 2), owners - 2)
        recv[me] = pair(me)

        done = ring_until(done, needed(layer))
        done = feed(done, 2)
        pick = jnp.where(
            lax.broadcasted_iota(jnp.int32, (BLK, 128), 0) == layer, 1.0, 0.0
        ).astype(jnp.bfloat16)

        def near_group(g, c):
            joined, packed = [], []
            for i in range(GROUP):
                j = g * GROUP + i
                near = [act[tabs[layer, k, per + j]] for k in range(3)]
                joined.append(jnp.concatenate(near + [pick], axis=0))
                w = wbuf[layer, j]
                packed.append(
                    jnp.concatenate(
                        [w[:, :128], jnp.where(low_lanes, w[:, 128:], btr[j])], axis=1
                    )
                )
            sums = [
                jnp.dot(p, x, preferred_element_type=jnp.float32) for p, x in zip(packed, joined)
            ]
            for i in range(GROUP):
                total[g * GROUP + i] = sums[i]
            return c

        groups = per // GROUP

        lax.fori_loop(0, groups // 2, near_group, 0)
        done = feed(done, 3)
        lax.fori_loop(groups // 2, groups, near_group, 0)
        done = feed(done, 7)
        for i in range(4):
            got = recv.at[pl.ds(0, batch - 1 if i == 3 else batch)]
            pltpu.make_async_copy(got, got, a2a_recv.at[now, i]).wait()

        def far_group(g, c):
            pairs, straights, sums, done = [], [], [], []
            for i in range(GROUP):
                j = g * GROUP + i
                pairs.append(recv[tabs[layer, 3, per + j]])
                slot = jnp.zeros((BLK, 128), jnp.int32) + tabs[layer, 4, per + j]
                straights.append(low_lanes == (slot == 0))
            for i in range(GROUP):
                joined = jnp.concatenate([jnp.zeros((BLK, 128), jnp.bfloat16), pairs[i]], axis=0)
                w = wbuf[layer, g * GROUP + i][:, 128:]
                sums.append(jnp.dot(w, joined, preferred_element_type=jnp.float32))
            for i in range(GROUP):
                far = jnp.where(straights[i], sums[i], pltpu.roll(sums[i], BLK, 1))
                z = total[g * GROUP + i] + far
                done.append(jnp.minimum(jnp.maximum(z, 0.0), 32.0).astype(jnp.bfloat16))
            for i in range(GROUP):
                after[g * GROUP + i] = done[i]
            return c

        lax.fori_loop(0, groups // 2, far_group, 0)
        done = feed(done, 8)
        lax.fori_loop(groups // 2, groups, far_group, 0)
        return done

    def two_layers(i, done):
        done = one_layer(2 * i, 0, done)
        return one_layer(2 * i + 1, 1, done)

    done = lax.fori_loop(0, layers // 2, two_layers, done)
    ring_until(done, end)
    for i in range(per // 2):
        part = act_even[2 * i : 2 * i + 2].reshape(128, 128).astype(jnp.float32).T
        o_ref[:, :, i * 128 : (i + 1) * 128] = (
            part[:rows].reshape(o_ref.shape[0], -1, 128).astype(jnp.bfloat16)
        )

    for par in range(2):
        sent = send.at[par, pl.ds(0, owners - 1)]
        pltpu.make_async_copy(sent, sent, a2a_send.at[par]).wait()

    for side in (0, 1):
        for t in range(own):
            count = (first, second)[t][side] * UNIT
            sent = wbuf.at[pl.ds(0, last), pl.ds(0, count)]
            pltpu.make_async_copy(sent, sent, ring_send.at[side, t]).wait()
    out = tall.at[pl.ds(0, layers - own)]
    pltpu.make_async_copy(out, out, small_send.at[0]).wait()
    out = ball.at[pl.ds(0, layers - own)]
    pltpu.make_async_copy(out, out, small_send.at[1]).wait()


def local(samples, weights, biases, near_blocks, remote_cols):
    batches, rows, width = samples.shape
    sections = lax.axis_size("segment")
    owners = lax.axis_size("neuron")
    per = width // BLK
    own = weights.shape[0]
    layers = own * sections
    share = rows // sections
    count = batches * share
    dims = (sections, owners, per, layers, count)
    bf16, f32 = jnp.bfloat16, jnp.float32
    return pl.pallas_call(
        functools.partial(kernel, dims),
        out_shape=jax.ShapeDtypeStruct((batches, share, width), bf16),
        in_specs=[
            pl.BlockSpec(memory_space=pltpu.HBM),
            pl.BlockSpec(memory_space=pltpu.HBM),
            pl.BlockSpec(memory_space=pltpu.VMEM),
            pl.BlockSpec(memory_space=pltpu.VMEM),
            pl.BlockSpec(memory_space=pltpu.VMEM),
        ],
        out_specs=pl.BlockSpec(memory_space=pltpu.VMEM),
        scratch_shapes=[
            pltpu.VMEM((batches, share, width), bf16),
            pltpu.VMEM((per, BLK, 128), bf16),
            pltpu.VMEM((per, BLK, 128), bf16),
            pltpu.VMEM((per, BLK, 128), f32),
            pltpu.VMEM((2, owners, BLK, 128), bf16),
            pltpu.VMEM((owners, BLK, 128), bf16),
            pltpu.VMEM((owners, BLK, 128), bf16),
            pltpu.VMEM((layers, per, BLK, 256), bf16),
            pltpu.VMEM((layers, width // 128, 128), f32),
            pltpu.VMEM((per, BLK, 128), bf16),
            pltpu.VMEM((layers, remote_cols.shape[1] // 128, 128), jnp.int32),
            pltpu.SMEM((layers, remote_cols.shape[1] // 128, 128), jnp.int32),
            pltpu.SemaphoreType.DMA((3,)),
            pltpu.SemaphoreType.DMA((2,)),
            pltpu.SemaphoreType.DMA((2,)),
            pltpu.SemaphoreType.DMA((2,)),
            pltpu.SemaphoreType.DMA((2, 4)),
            pltpu.SemaphoreType.DMA((2, own)),
            pltpu.SemaphoreType.DMA((2, sections, own * per // UNIT)),
        ],
        compiler_params=pltpu.CompilerParams(
            collective_id=0, has_side_effects=True, vmem_limit_bytes=62 * 1024 * 1024
        ),
    )(
        samples,
        weights.reshape(own, per, BLK, 256),
        biases,
        near_blocks.transpose(2, 0, 1),
        remote_cols,
    )


def solution(mesh):
    return jax.shard_map(
        local,
        mesh=mesh,
        in_specs=(
            P(None, None, "neuron"),
            P("segment", "neuron", None),
            P("segment", "neuron"),
            P("segment", "neuron", None),
            P("segment", None),
        ),
        out_specs=P(None, "segment", "neuron"),
        check_vma=False,
    )
```

```python
import functools
import math

import jax
import jax.numpy as jnp
from jax import lax
from jax.experimental import pallas as pl
from jax.experimental.pallas import tpu as pltpu
from jax.sharding import PartitionSpec as P

MESH = pl.DeviceIdType.MESH
BLK = 64
UNIT = 2
FIRST_SHARE = 8
SECOND_SHARE = 7
SKEW = 3
LEAD = 31
BEHIND = 5
GROUP = 16


def table(cols, per, me, roll):
    rows = cols.shape[0]
    many = 128 // per
    lane = lax.broadcasted_iota(jnp.int32, (rows, 128), 1)
    row = lax.broadcasted_iota(jnp.int32, (rows, 128), 0)
    key = lax.rem(lane, per) * per + lax.rem(cols, per)
    asked = cols // per == me
    result = jnp.zeros((rows, 128), jnp.int32)
    for g in range(many):
        here = asked & (lane // per == g)
        low = jnp.min(jnp.where(here, key, per * per - 1), axis=1, keepdims=True)
        high = jnp.max(jnp.where(here, key, 0), axis=1, keepdims=True)
        result = jnp.where(lane == g, lax.rem(low, per), result)
        result = jnp.where(lane == many + g, lax.rem(high, per), result)
    mine = jnp.sum(jnp.where(row == me // many, cols // per, 0), axis=0, keepdims=True)
    mine = jnp.zeros((rows, 128), jnp.int32) + mine
    mine = roll(mine, lax.rem(per - per * lax.rem(me, many) + 128, 128))
    slot = jnp.zeros((rows, 128), jnp.int32)
    for k in range(1, per):
        slot = jnp.where((roll(mine, k) == mine) & (lane >= per + k), 1, slot)
    far = (lane >= per) & (lane < 2 * per)
    result = jnp.where(far & (row == 3), mine, result)
    return jnp.where(far & (row == 4), slot, result)


def kernel(
    dims, x_ref, w_ref, b_ref, near_ref, cols_ref, o_ref,
    x_in,
    act_even, act_odd, total, send, recv_even, recv_odd, wbuf, ball, btr, tall, tabs,
    local_sem, small_send, small_recv, a2a_send, a2a_recv, ring_send, ring_recv,
):
    sections, owners, per, layers, rows = dims
    own = layers // sections
    s = lax.axis_index("segment")
    me = lax.axis_index("neuron")
    ahead = lax.rem(s + 1, sections)
    behind = lax.rem(s + sections - 1, sections)
    last = sections - 1

    barrier = pltpu.get_barrier_semaphore()

    def greet(d, carry):
        pl.semaphore_signal(
            barrier, inc=1, device_id={"neuron": lax.rem(me + d, owners)}, device_id_type=MESH
        )
        return carry

    lax.fori_loop(1, owners, greet, 0)

    def greet_section(d, carry):
        pl.semaphore_signal(
            barrier, inc=1, device_id={"segment": lax.rem(s + d, sections)}, device_id_type=MESH
        )
        return carry

    lax.fori_loop(1, sections, greet_section, 0)

    share_rows = rows // x_in.shape[0]
    mine = x_ref.at[:, pl.ds(pl.multiple_of(s * share_rows, share_rows), share_rows)]
    loads = [
        pltpu.make_async_copy(mine, x_in, local_sem.at[0]),
        pltpu.make_async_copy(w_ref, wbuf.at[pl.ds(s * own, own)], local_sem.at[1]),
    ]
    for load in loads:
        load.start()
    pl.semaphore_wait(barrier, owners - 1 + sections - 1)

    units = per // UNIT
    first = (FIRST_SHARE, units - FIRST_SHARE)
    second = (SECOND_SHARE, units - SECOND_SHARE)
    window = (first[0] + second[0], first[1] + second[1])
    lone = window[0] - SKEW
    end = window[1] * sections

    def ring(home, i, side):
        later = (i >= first[side]).astype(jnp.int32)
        begin = 0 if side == 0 else first[0] + later * (second[0] - first[0])
        place = begin + i - later * first[side]
        at = pl.ds(place * UNIT, UNIT)
        layer = home * own + later
        return pltpu.make_async_remote_copy(
            src_ref=wbuf.at[layer, at], dst_ref=wbuf.at[layer, at],
            send_sem=ring_send.at[side, later], recv_sem=ring_recv.at[side, home, i],
            device_id={"segment": (ahead, behind)[side]}, device_id_type=MESH,
        )

    def hand_on(side, home, i, fine, hops):
        home, i = jnp.clip(home, 0, last), jnp.clip(i, 0, window[side] - 1)
        copy = ring(home, i, side)

        @pl.when(fine)
        def _():
            copy.wait_recv()

        @pl.when(fine & (hops < last))
        def _():
            copy.start()

    own_base = jnp.where(s == last, SKEW * (last - 1), window[0] * s)
    own_early = jnp.where(s == 0, window[1], jnp.minimum(window[1], SKEW * (sections - s)))
    own_late = window[1] * (s - 1) + SKEW * (sections - s) - own_early

    def give_own(side, i, fine):
        @pl.when(fine)
        def _():
            i_in = jnp.clip(i, 0, window[side] - 1)
            ring(s, i_in, side).start()

    def ring_step(e):
        t = e - own_base
        give_own(0, jnp.where(e < SKEW, e, t), (e < SKEW) | ((t >= SKEW) & (t < window[0])))
        t = e - own_late
        give_own(
            1,
            jnp.where(e < own_early, e, t),
            (e < own_early) | ((s > 0) & (t >= own_early) & (t < window[1])),
        )

        inner = (e >= SKEW) & (e < SKEW * s)
        home = jnp.where(inner, s - e // SKEW, -1)
        i = lax.rem(e, SKEW)
        t = e - SKEW * s
        fits = (s >= 1) & (t >= 0) & (t < window[0])
        home, i = jnp.where(fits, 0, home), jnp.where(fits, t, i)
        t = t - window[0]
        fits = (t >= 0) & (t < lone * (s - 1))
        t = jnp.maximum(t, 0)
        home = jnp.where(fits, 1 + t // lone, home)
        i = jnp.where(fits, SKEW + lax.rem(t, lone), i)
        t = e - window[0] * (s + 1)
        fits = (t >= 0) & (t < SKEW * (last - 1 - s))
        t_in = jnp.maximum(t, 0)
        home = jnp.where(fits, last - 1 - t_in // SKEW, home)
        i = jnp.where(fits, lax.rem(t_in, SKEW), i)
        t = t - SKEW * (last - 1 - s)
        fits = (s < last) & (t >= 0) & (t < window[0])
        home, i = jnp.where(fits, last, home), jnp.where(fits, t, i)
        hand_on(0, home, i, home >= 0, lax.rem(s - home + sections, sections))

        t = e - SKEW * (sections + 1 + s)
        t_in = jnp.maximum(t, 0)
        home = t_in // lone
        fine = (t >= 0) & (home > s) & (home < last)
        hand_on(0, home, SKEW + lax.rem(t_in, lone), fine, s - home + sections)

        for t, low, high, hops in (
            (e - SKEW * (sections - s), 0, s, sections - s),
            (e + SKEW * s, s + 1, sections, -s),
        ):
            t_in = jnp.maximum(t, 0)
            home = t_in // window[1]
            fine = (t >= 0) & (home >= low) & (home < high)
            hand_on(1, home, lax.rem(t_in, window[1]), fine, home + hops)

    def ring_until(low, high):
        def one(e, carry):
            ring_step(e)
            return carry

        lax.fori_loop(low, high, one, 0)
        return jnp.maximum(low, high)

    def needed(layer):
        return jnp.minimum(LEAD + layer * (end + BEHIND - LEAD) // (layers - 1), end)

    def own_table(t):
        cols = jnp.concatenate(
            [cols_ref[t : t + 1, r : r + 128] for r in range(0, cols_ref.shape[1], 128)], axis=0
        )
        tall[s * own + t] = table(cols, per, me, lambda v, k: pltpu.roll(v, k, 1))
        for k in range(3):
            tall[s * own + t, k : k + 1, per : 2 * per] = near_ref[k, t : t + 1, :]
        for i in range(per // 2):
            ball[s * own + t, i : i + 1, :] = b_ref[t : t + 1, i * 128 : (i + 1) * 128].astype(
                jnp.float32
            )

    def share(d, carry):
        to = {"segment": lax.rem(s + d, sections)}
        pltpu.make_async_remote_copy(
            src_ref=tall.at[pl.ds(s * own, own)], dst_ref=tall.at[pl.ds(s * own, own)],
            send_sem=small_send.at[0], recv_sem=small_recv.at[0],
            device_id=to, device_id_type=MESH,
        ).start()
        pltpu.make_async_remote_copy(
            src_ref=ball.at[pl.ds(s * own, own)], dst_ref=ball.at[pl.ds(s * own, own)],
            send_sem=small_send.at[1], recv_sem=small_recv.at[1],
            device_id=to, device_id_type=MESH,
        ).start()
        return carry


    def bias_columns(i):
        rows_of = jnp.concatenate(
            [
                jnp.zeros((BLK, 128), jnp.float32),
                ball[:, i, :],
                jnp.zeros((BLK - layers, 128), jnp.float32),
            ],
            axis=0,
        )
        btr[2 * i : 2 * i + 2] = rows_of.T.astype(jnp.bfloat16).reshape(2, BLK, 128)

    def take_samples(i):
        part = x_in[:, :, i * 128 : (i + 1) * 128].reshape(rows, 128).astype(jnp.float32)
        part = jnp.concatenate([part, part], axis=0).T.astype(jnp.bfloat16)
        act_even[2 * i : 2 * i + 2] = part.reshape(2, BLK, 128)

    loads[1].wait()
    done = ring_until(0, SKEW)
    for t in range(own):
        own_table(t)
        done = ring_until(done, done + 1)
    lax.fori_loop(1, sections, share, 0)
    loads[0].wait()
    for i in range(per // 2):
        take_samples(i)
        if i % 4 == 3:
            done = ring_until(done, done + 1)
    pltpu.make_async_copy(
        tall.at[pl.ds(0, layers - own)], tall.at[pl.ds(0, layers - own)], small_recv.at[0]
    ).wait()
    table_load = pltpu.make_async_copy(tall, tabs, local_sem.at[2])
    table_load.start()
    pltpu.make_async_copy(
        ball.at[pl.ds(0, layers - own)], ball.at[pl.ds(0, layers - own)], small_recv.at[1]
    ).wait()
    for i in range(per // 2):
        bias_columns(i)
        if i % 4 == 3:
            done = ring_until(done, done + 1)
    table_load.wait()

    low_lanes = lax.broadcasted_iota(jnp.int32, (BLK, 128), 1) < BLK
    batch = owners // 4
    many = 128 // per
    chips, chip = owners // 2, me // 2
    side = math.isqrt(chips)

    def distance(offset):
        return sum(min(d, side - d) for d in divmod(offset, side))

    ranked = sorted(range(1, chips), key=lambda o: (-distance(o), o % side == 0 or o < side))
    order = []
    for begin in range(0, chips - 1, 5):
        taken = ranked[begin : begin + 5]
        order.append((begin, len(taken), sum(o * chips**i for i, o in enumerate(taken))))

    def one_layer(layer, now, done):
        act, after = (act_even, act_odd)[now], (act_odd, act_even)[now]
        recv = (recv_even, recv_odd)[now]
        begin = begin_steps = jnp.maximum(done, needed(layer))
        steps = jnp.maximum(needed(jnp.minimum(layer + 1, layers - 1)) - begin, 0)

        def feed(done, portion):
            return ring_until(done, begin + steps * portion // 8)


        @pl.when(layer >= 2)
        def _():
            sent = send.at[now, pl.ds(0, owners - 1)]
            pltpu.make_async_copy(sent, sent, a2a_send.at[now]).wait()

        def pair(q):
            first = tabs[layer, q // many, lax.rem(q, many)]
            second = tabs[layer, q // many, many + lax.rem(q, many)]
            return jnp.where(low_lanes, act[first], act[second])

        def give(q, number):
            send[now, q] = pair(q)
            pltpu.make_async_remote_copy(
                src_ref=send.at[now, q], dst_ref=recv.at[me],
                send_sem=a2a_send.at[now], recv_sem=a2a_recv.at[now, number // batch],
                device_id={"neuron": q}, device_id_type=MESH,
            ).start()

        def give_chip(number, packed):
            offset, packed = lax.rem(packed, chips), packed // chips
            x = lax.rem(chip // side + offset // side, side)
            y = lax.rem(chip + offset, side)
            for core in range(2):
                q = (x * side + y) * 2 + lax.rem(me + core, 2)
                give(q, number * 2 + core)
            return packed

        for place, amount, packed in order:
            lax.fori_loop(place, place + amount, give_chip, jnp.int32(packed))
            if place == 5:
                done = ring_until(done, jnp.where(layer > 0, begin_steps + steps // 8, 0))
        give(me + 1 - 2 * lax.rem(me, 2), owners - 2)
        recv[me] = pair(me)

        done = ring_until(done, needed(layer))
        done = feed(done, 2)
        pick = jnp.where(
            lax.broadcasted_iota(jnp.int32, (BLK, 128), 0) == layer, 1.0, 0.0
        ).astype(jnp.bfloat16)

        def near_group(g, c):
            joined, packed = [], []
            for i in range(GROUP):
                j = g * GROUP + i
                near = [act[tabs[layer, k, per + j]] for k in range(3)]
                joined.append(jnp.concatenate(near + [pick], axis=0))
                w = wbuf[layer, j]
                packed.append(
                    jnp.concatenate(
                        [w[:, :128], jnp.where(low_lanes, w[:, 128:], btr[j])], axis=1
                    )
                )
            sums = [
                jnp.dot(p, x, preferred_element_type=jnp.float32) for p, x in zip(packed, joined)
            ]
            for i in range(GROUP):
                total[g * GROUP + i] = sums[i]
            return c

        groups = per // GROUP

        lax.fori_loop(0, groups // 2, near_group, 0)
        done = feed(done, 3)
        lax.fori_loop(groups // 2, groups, near_group, 0)
        done = feed(done, 6)
        for i in range(4):
            got = recv.at[pl.ds(0, batch - 1 if i == 3 else batch)]
            pltpu.make_async_copy(got, got, a2a_recv.at[now, i]).wait()

        def far_group(g, c):
            pairs, straights, sums, done = [], [], [], []
            for i in range(GROUP):
                j = g * GROUP + i
                pairs.append(recv[tabs[layer, 3, per + j]])
                slot = jnp.zeros((BLK, 128), jnp.int32) + tabs[layer, 4, per + j]
                straights.append(low_lanes == (slot == 0))
            for i in range(GROUP):
                joined = jnp.concatenate([jnp.zeros((BLK, 128), jnp.bfloat16), pairs[i]], axis=0)
                w = wbuf[layer, g * GROUP + i][:, 128:]
                sums.append(jnp.dot(w, joined, preferred_element_type=jnp.float32))
            for i in range(GROUP):
                far = jnp.where(straights[i], sums[i], pltpu.roll(sums[i], BLK, 1))
                z = total[g * GROUP + i] + far
                done.append(jnp.minimum(jnp.maximum(z, 0.0), 32.0).astype(jnp.bfloat16))
            for i in range(GROUP):
                after[g * GROUP + i] = done[i]
            return c

        lax.fori_loop(0, groups // 2, far_group, 0)
        done = feed(done, 7)
        lax.fori_loop(groups // 2, groups, far_group, 0)
        return feed(done, 8)

    def two_layers(i, done):
        done = one_layer(2 * i, 0, done)
        return one_layer(2 * i + 1, 1, done)

    done = lax.fori_loop(0, layers // 2, two_layers, done)
    ring_until(done, end)
    for i in range(per // 2):
        part = act_even[2 * i : 2 * i + 2].reshape(128, 128).astype(jnp.float32).T
        o_ref[:, :, i * 128 : (i + 1) * 128] = (
            part[:rows].reshape(o_ref.shape[0], -1, 128).astype(jnp.bfloat16)
        )

    for par in range(2):
        sent = send.at[par, pl.ds(0, owners - 1)]
        pltpu.make_async_copy(sent, sent, a2a_send.at[par]).wait()

    for side in (0, 1):
        for t in range(own):
            count = (first, second)[t][side] * UNIT
            sent = wbuf.at[pl.ds(0, last), pl.ds(0, count)]
            pltpu.make_async_copy(sent, sent, ring_send.at[side, t]).wait()
    out = tall.at[pl.ds(0, layers - own)]
    pltpu.make_async_copy(out, out, small_send.at[0]).wait()
    out = ball.at[pl.ds(0, layers - own)]
    pltpu.make_async_copy(out, out, small_send.at[1]).wait()


def local(samples, weights, biases, near_blocks, remote_cols):
    batches, rows, width = samples.shape
    sections = lax.axis_size("segment")
    owners = lax.axis_size("neuron")
    per = width // BLK
    own = weights.shape[0]
    layers = own * sections
    share = rows // sections
    count = batches * share
    dims = (sections, owners, per, layers, count)
    bf16, f32 = jnp.bfloat16, jnp.float32
    return pl.pallas_call(
        functools.partial(kernel, dims),
        out_shape=jax.ShapeDtypeStruct((batches, share, width), bf16),
        in_specs=[
            pl.BlockSpec(memory_space=pltpu.HBM),
            pl.BlockSpec(memory_space=pltpu.HBM),
            pl.BlockSpec(memory_space=pltpu.VMEM),
            pl.BlockSpec(memory_space=pltpu.VMEM),
            pl.BlockSpec(memory_space=pltpu.VMEM),
        ],
        out_specs=pl.BlockSpec(memory_space=pltpu.VMEM),
        scratch_shapes=[
            pltpu.VMEM((batches, share, width), bf16),
            pltpu.VMEM((per, BLK, 128), bf16),
            pltpu.VMEM((per, BLK, 128), bf16),
            pltpu.VMEM((per, BLK, 128), f32),
            pltpu.VMEM((2, owners, BLK, 128), bf16),
            pltpu.VMEM((owners, BLK, 128), bf16),
            pltpu.VMEM((owners, BLK, 128), bf16),
            pltpu.VMEM((layers, per, BLK, 256), bf16),
            pltpu.VMEM((layers, width // 128, 128), f32),
            pltpu.VMEM((per, BLK, 128), bf16),
            pltpu.VMEM((layers, remote_cols.shape[1] // 128, 128), jnp.int32),
            pltpu.SMEM((layers, remote_cols.shape[1] // 128, 128), jnp.int32),
            pltpu.SemaphoreType.DMA((3,)),
            pltpu.SemaphoreType.DMA((2,)),
            pltpu.SemaphoreType.DMA((2,)),
            pltpu.SemaphoreType.DMA((2,)),
            pltpu.SemaphoreType.DMA((2, 4)),
            pltpu.SemaphoreType.DMA((2, own)),
            pltpu.SemaphoreType.DMA((2, sections, own * per // UNIT)),
        ],
        compiler_params=pltpu.CompilerParams(
            collective_id=0, has_side_effects=True, vmem_limit_bytes=62 * 1024 * 1024
        ),
    )(
        samples,
        weights.reshape(own, per, BLK, 256),
        biases,
        near_blocks.transpose(2, 0, 1),
        remote_cols,
    )


def solution(mesh):
    return jax.shard_map(
        local,
        mesh=mesh,
        in_specs=(
            P(None, None, "neuron"),
            P("segment", "neuron", None),
            P("segment", "neuron"),
            P("segment", "neuron", None),
            P("segment", None),
        ),
        out_specs=P(None, "segment", "neuron"),
        check_vma=False,
    )
```
